32 devices in a mesh: groups: 2 (over x), row: 8 (over z, y), col: 2 (over core).
Axes of the slice: x: 2, y: 2, z: 4, core: 2. Of those that a mesh axis runs over, the one named last changes fastest.
Arguments:
- tokens: bfloat16 [1024, 8192], P(('groups', 'row'), 'col'), parts along dimension 0, may hold values from -6 to 6
- gate_weight: bfloat16 [8192, 14336], P('col', 'row'), may hold values from -0.125 to 0.125
- up_weight: bfloat16 [8192, 14336], P('col', 'row'), may hold values from -0.125 to 0.125
- down_weight: bfloat16 [14336, 8192], P('row', 'col'), may hold values from -0.09375 to 0.09375
- gate_mask: int32 [64, 112], P('col', 'row'), may hold values from 0 to 1, as said below
- up_mask: int32 [64, 112], P('col', 'row'), may hold values from 0 to 1, as said below
- down_mask: int32 [112, 64], P('row', 'col'), may hold values from 0 to 1, as said below
Outputs:
- mixed: bfloat16 [1024, 8192], P(('groups', 'row'), 'col'), parts along dimension 0
The draws below stay inside these ranges and needn't reach their ends.
There are 2 independent parts, one for each index of `groups`. The reference program is written for one: setup_inputs(seed, part) draws one part's arguments, and reference() takes and returns one part's arrays. A program takes and returns all parts, laid end to end along the dimension named above; an argument that names none is the same for every part. Nothing has to cross between parts.
Inputs may be any that keep to these rules, and one draw needn't show every extreme that they name: `gate_mask`: 1 keeps the 128 x 128 block of the matching projection, 0 prunes it. `up_mask`: 1 keeps the 128 x 128 block of the matching projection, 0 prunes it. `down_mask`: 1 keeps the 128 x 128 block of the matching projection, 0 prunes it.
All inputs are finite; a program needn't handle non-finite values.
Results may differ from the reference program's by a relative error of at most 0.0049.
Values may be sent and summed in bfloat16 or wider, within the bound.
No kernel may reach another device: no remote copies, remote signals or barrier semaphores. Data moves between devices by JAX's collectives and lax.ppermute only.
A program may use at most 192 MiB of HBM per device.

```python
import jax
import jax.numpy as jnp

D = 8192
FF = 14336
BLOCK = 128
TOKENS = 512


def column_levels(key):
    return jax.random.randint(key, (FF // BLOCK,), 20, 480)


def draw_gate_mask(key, part):
    levels = column_levels(key)
    key = jax.random.fold_in(key, 11)
    scores = jax.random.randint(key, (D // BLOCK, FF // BLOCK), 0, 1000)
    return (scores < levels[None, :]).astype(jnp.int32)


def draw_up_mask(key, part):
    levels = column_levels(key)
    key = jax.random.fold_in(key, 12)
    scores = jax.random.randint(key, (D // BLOCK, FF // BLOCK), 0, 1000)
    return (scores < levels[None, :]).astype(jnp.int32)


def draw_down_mask(key, part):
    levels = column_levels(key)
    key = jax.random.fold_in(key, 13)
    scores = jax.random.randint(key, (FF // BLOCK, D // BLOCK), 0, 1000)
    return (scores < levels[:, None]).astype(jnp.int32)


def steps_of(key, dims, cuts, least, largest):
    def one(dim, blocks):
        draws = jax.random.uniform(jax.random.fold_in(jax.random.fold_in(key, 6), dim), (blocks,), jnp.float32, least / len(cuts), largest / len(cuts))
        return jnp.repeat(jnp.exp(draws), dims[dim] // blocks).reshape((-1,) + (1,) * (len(dims) - dim - 1))

    level = one(*cuts[0])
    for cut in cuts[1:]:
        level = level * one(*cut)
    return level


def gaussian(rng, shape, width, limit, cuts=(), kind=jnp.bfloat16):
    loudness = steps_of(rng, shape, cuts, -0.22, 0.18) if cuts else 1.0
    entries = jax.random.normal(rng, shape, jnp.float32) * width * loudness
    return jnp.minimum(jnp.maximum(entries, -limit), limit).astype(kind)


def setup_inputs(seed: int = 0, part: int = 0) -> dict:
    key_list = jax.random.split(jax.random.key(seed), 8)
    own_keys = jax.random.split(jax.random.fold_in(key_list[7], part), 8)
    return {
        "tokens": gaussian(own_keys[0], (TOKENS, D), 1.0, 6.0, ((0, 8), (1, 2))),
        "gate_weight": gaussian(key_list[1], (D, FF), (D // 4) ** -0.5, 0.125, ((0, 2), (1, 8))),
        "up_weight": gaussian(key_list[2], (D, FF), (D // 4) ** -0.5, 0.125, ((0, 2), (1, 8))),
        "down_weight": gaussian(key_list[3], (FF, D), (FF // 4) ** -0.5, 0.09375, ((0, 8), (1, 2))),
        "gate_mask": draw_gate_mask(jax.random.fold_in(key_list[7], 71), part),
        "up_mask": draw_up_mask(jax.random.fold_in(key_list[7], 71), part),
        "down_mask": draw_down_mask(jax.random.fold_in(key_list[7], 71), part),
    }


def expand_mask(mask, weight):
    blocks_down, blocks_across = mask.shape
    side_down = weight.shape[0] // blocks_down
    side_across = weight.shape[1] // blocks_across
    spread = jnp.broadcast_to(mask[:, None, :, None], (blocks_down, side_down, blocks_across, side_across))
    return weight * spread.reshape(weight.shape).astype(weight.dtype)


def reference(tokens, gate_weight, up_weight, down_weight, gate_mask, up_mask, down_mask):
    gate_kept = expand_mask(gate_mask, gate_weight)
    up_kept = expand_mask(up_mask, up_weight)
    down_kept = expand_mask(down_mask, down_weight)
    gate = jnp.dot(tokens, gate_kept, preferred_element_type=jnp.float32)
    up = jnp.dot(tokens, up_kept, preferred_element_type=jnp.float32)
    hidden = (jax.nn.silu(gate) * up).astype(jnp.bfloat16)
    return jnp.dot(hidden, down_kept, preferred_element_type=jnp.float32).astype(jnp.bfloat16)
```

```python
import functools

import jax
import jax.numpy as jnp
from jax import lax
from jax.experimental import pallas as pl
from jax.experimental.pallas import tpu as pltpu
from jax.sharding import PartitionSpec as P

SIDE = 128
UNROLL = 4
SLOTS = 8
CHUNKS = 2
F32 = jnp.float32
BF16 = jnp.bfloat16


def list_kernel(*refs):
    masks, (index, count) = refs[:-2], refs[-2:]
    at = 0
    for mask in masks:
        deep, wide = mask.shape

        def column(j, _, mask=mask, deep=deep, at=at):
            def row(i, n):
                index[at + j, n] = i
                return n + jnp.where(mask[i, j] != 0, 1, 0)

            n = lax.fori_loop(0, deep, row, 0)
            for t in range(UNROLL):
                index[at + j, n + t] = 0
            count[0, at + j] = n
            return 0

        lax.fori_loop(0, wide, column, 0)
        at += wide


def kept_lists(*masks):
    deep = masks[0].shape[0]
    wide = sum(m.shape[1] for m in masks)
    smem = pl.BlockSpec(memory_space=pltpu.SMEM)
    return pl.pallas_call(
        list_kernel,
        out_shape=(
            jax.ShapeDtypeStruct((wide, deep + UNROLL), jnp.int32),
            jax.ShapeDtypeStruct((1, wide), jnp.int32),
        ),
        in_specs=[smem] * len(masks),
        out_specs=(smem, smem),
    )(*masks)


def fetch_column(j, index, count, columns, weights, slots, sems, go):
    slot = lax.rem(j, SLOTS)
    per, first, offset = columns
    for w, weight in enumerate(weights):

        @pl.when(j // per == w)
        def _(w=w, weight=weight):
            here = first + lax.rem(j, per)
            listed = w * offset + here

            def one(t, _):
                i = index[listed, t]
                copy = pltpu.make_async_copy(
                    weight.at[pl.ds(pl.multiple_of(i * SIDE, SIDE), SIDE), pl.ds(pl.multiple_of(here * SIDE, SIDE), SIDE)],
                    slots.at[slot, pl.ds(pl.multiple_of(t * SIDE, SIDE), SIDE), :],
                    sems.at[slot],
                )
                if go:
                    copy.start()
                else:
                    copy.wait()
                return 0

            lax.fori_loop(0, count[0, listed], one, 0)


def multiply_column(j, index, count, columns, held, slots, out):
    slot = lax.rem(j, SLOTS)
    per, first, offset = columns
    listed = (j // per) * offset + first + lax.rem(j, per)
    n = count[0, listed]
    rows = held.shape[0]
    for t in range(UNROLL - 1):
        slots[slot, pl.ds(pl.multiple_of((n + t) * SIDE, SIDE), SIDE), :] = jnp.zeros((SIDE, SIDE), BF16)

    def step(s, total):
        lhs = jnp.concatenate(
            [held[:, pl.ds(pl.multiple_of(index[listed, s * UNROLL + t] * SIDE, SIDE), SIDE)] for t in range(UNROLL)],
            axis=1,
        )
        deep = UNROLL * SIDE
        rhs = slots[slot, pl.ds(pl.multiple_of(s * deep, deep), deep), :]
        return total + jnp.dot(lhs, rhs, preferred_element_type=F32)

    out[...] = lax.fori_loop(0, (n + UNROLL - 1) // UNROLL, step, jnp.zeros((rows, SIDE), F32)).astype(out.dtype)


def gate_up_kernel(columns, places, index, count, *refs):
    pieces = refs[: len(places)]
    gate, up, out, held, slots, sems, piece_sems = refs[len(places) :]
    j = pl.program_id(0)
    wide = pl.num_programs(0)
    fetch = functools.partial(fetch_column, index=index, count=count, columns=columns, weights=(gate, up), slots=slots, sems=sems)
    copies = [
        pltpu.make_async_copy(
            piece, held.at[pl.ds(row, piece.shape[0]), pl.ds(column, piece.shape[1])], piece_sems.at[k]
        )
        for k, (piece, (row, column)) in enumerate(zip(pieces, places))
    ]

    @pl.when(j == 0)
    def _():
        for copy in copies:
            copy.start()
        lax.fori_loop(0, jnp.minimum(SLOTS - 1, wide), lambda k, _: (fetch(k, go=True), 0)[1], 0)
        for copy in copies:
            copy.wait()

    @pl.when(j + SLOTS - 1 < wide)
    def _():
        fetch(j + SLOTS - 1, go=True)

    fetch(j, go=False)
    multiply_column(j, index, count, columns, held, slots, out)


def gate_up(index, count, pieces, places, gate, up, first, blocks):
    deep, width = gate.shape
    rows = max(row + piece.shape[0] for piece, (row, _) in zip(pieces, places))
    wide = 2 * blocks
    return pl.pallas_call(
        functools.partial(gate_up_kernel, (blocks, first, width // SIDE), places),
        out_shape=jax.ShapeDtypeStruct((rows, wide * SIDE), F32),
        grid_spec=pltpu.PrefetchScalarGridSpec(
            num_scalar_prefetch=2,
            grid=(wide,),
            in_specs=[pl.BlockSpec(memory_space=pl.ANY)] * (len(pieces) + 2),
            out_specs=pl.BlockSpec((rows, SIDE), lambda j, *_: (0, j)),
            scratch_shapes=[
                pltpu.VMEM((rows, deep), BF16),
                pltpu.VMEM((SLOTS, deep + (UNROLL - 1) * SIDE, SIDE), BF16),
                pltpu.SemaphoreType.DMA((SLOTS,)),
                pltpu.SemaphoreType.DMA((len(pieces),)),
            ],
        ),
        compiler_params=pltpu.CompilerParams(vmem_limit_bytes=40 << 20),
        cost_estimate=pl.CostEstimate(
            flops=rows * deep * wide * SIDE, bytes_accessed=deep * wide * SIDE, transcendentals=0
        ),
    )(index, count, *pieces, gate, up)


def down_kernel(parts, blocks, index, count, *refs):
    sums = refs[: 2 * parts]
    down, out, held, slots, sems, mine, other, sum_sems = refs[2 * parts :]
    j = pl.program_id(0)
    wide = pl.num_programs(0)
    columns = (wide, 0, 0)
    fetch = functools.partial(fetch_column, index=index, count=count, columns=columns, weights=(down,), slots=slots, sems=sems)

    @pl.when(j == 0)
    def _():
        copies = []
        for k in range(parts):
            copies.append(
                (
                    pltpu.make_async_copy(sums[k], mine.at[k], sum_sems.at[2 * k]),
                    pltpu.make_async_copy(sums[parts + k], other.at[k], sum_sems.at[2 * k + 1]),
                )
            )
        for pair in copies:
            for copy in pair:
                copy.start()
        lax.fori_loop(0, jnp.minimum(SLOTS - 1, wide), lambda k, _: (fetch(k, go=True), 0)[1], 0)
        width = blocks * SIDE
        rows = held.shape[0]
        for k, pair in enumerate(copies):
            for copy in pair:
                copy.wait()

            def some(r, _, k=k):
                at = pl.ds(pl.multiple_of(r * 16, 16), 16)
                gate = mine[k, at, :width] + other[k, at, :width]
                up = mine[k, at, width:] + other[k, at, width:]
                held[at, pl.ds(k * width, width)] = (gate / (1.0 + jnp.exp(-gate)) * up).astype(BF16)
                return 0

            lax.fori_loop(0, rows // 16, some, 0)

    @pl.when(j + SLOTS - 1 < wide)
    def _():
        fetch(j + SLOTS - 1, go=True)

    fetch(j, go=False)
    multiply_column(j, index, count, columns, held, slots, out)


def down_product(index, count, mine, other, down):
    deep, width = down.shape
    parts = len(mine)
    rows, both = mine[0].shape
    wide = width // SIDE
    return pl.pallas_call(
        functools.partial(down_kernel, parts, both // 2 // SIDE),
        out_shape=jax.ShapeDtypeStruct((rows, width), F32),
        grid_spec=pltpu.PrefetchScalarGridSpec(
            num_scalar_prefetch=2,
            grid=(wide,),
            in_specs=[pl.BlockSpec(memory_space=pl.ANY)] * (2 * parts + 1),
            out_specs=pl.BlockSpec((rows, SIDE), lambda j, *_: (0, j)),
            scratch_shapes=[
                pltpu.VMEM((rows, deep), BF16),
                pltpu.VMEM((SLOTS, deep + (UNROLL - 1) * SIDE, SIDE), BF16),
                pltpu.SemaphoreType.DMA((SLOTS,)),
                pltpu.VMEM((parts, rows, both), F32),
                pltpu.VMEM((parts, rows, both), F32),
                pltpu.SemaphoreType.DMA((2 * parts,)),
            ],
        ),
        compiler_params=pltpu.CompilerParams(vmem_limit_bytes=48 << 20),
        cost_estimate=pl.CostEstimate(
            flops=rows * deep * width, bytes_accessed=deep * width, transcendentals=rows * deep
        ),
    )(index, count, *mine, *other, down)


def ring_of(n):
    order = list(range(n)) if n > 8 else list(range(0, n, 2)) + list(range(n - 1, 0, -2))
    onward = [(order[k], order[(k + 1) % n]) for k in range(n)]
    return onward, [(b, a) for a, b in onward]


def gather(block, onward, back, n):
    behind, ahead = [block], [block]
    for _ in range(n // 2 - 1):
        behind.append(lax.ppermute(behind[-1], "row", onward))
        ahead.append(lax.ppermute(ahead[-1], "row", back))
    half = block.shape[1] // 2
    left = lax.ppermute(behind[-1][:, :half], "row", onward)
    right = lax.ppermute(ahead[-1][:, half:], "row", back)
    return behind + ahead[1:], (left, right)


def scatter(part, rows, onward, back, n):
    half = part.shape[1] // 2
    far = n // 2

    def block(k):
        at = 0 if k == 0 else (n - 1 if abs(k) == far else (-k if k < 0 else far - 1 + k))
        return part[at * rows : (at + 1) * rows]

    on = lax.ppermute(block(far)[:, :half].astype(BF16), "row", onward)
    ba = lax.ppermute(block(far)[:, half:].astype(BF16), "row", back)
    for k in range(far - 1, 0, -1):
        if k == far - 1:
            on_sum = jnp.concatenate((block(k)[:, :half] + on.astype(F32), block(k)[:, half:]), axis=1)
            ba_sum = jnp.concatenate((block(-k)[:, :half], block(-k)[:, half:] + ba.astype(F32)), axis=1)
        else:
            on_sum = block(k) + on.astype(F32)
            ba_sum = block(-k) + ba.astype(F32)
        on = lax.ppermute(on_sum.astype(BF16), "row", onward)
        ba = lax.ppermute(ba_sum.astype(BF16), "row", back)
    return (block(0) + on.astype(F32) + ba.astype(F32)).astype(BF16)


def body(n, tokens, gate, up, down, gate_mask, up_mask, down_mask):
    onward, back = ring_of(n)
    swap = [(0, 1), (1, 0)]
    rows = tokens.shape[0] // CHUNKS
    half = tokens.shape[1] // 2
    hidden_blocks = gate.shape[1] // SIDE
    index, count = kept_lists(gate_mask, up_mask)
    down_index, down_count = kept_lists(down_mask)

    cut = (hidden_blocks + 1) // 2
    spans = ((0, hidden_blocks),)
    outs = []
    for c in range(CHUNKS):
        blocks, (left, right) = gather(tokens[c * rows : (c + 1) * rows], onward, back, n)
        pieces = blocks + [left, right]
        places = [(k * rows, 0) for k in range(n - 1)] + [((n - 1) * rows, 0), ((n - 1) * rows, half)]
        mine = [gate_up(index, count, pieces, places, gate, up, first, some) for first, some in spans]
        other = [lax.ppermute(m, "col", swap) for m in mine]
        part = down_product(down_index, down_count, mine, other, down)
        outs.append(scatter(part, rows, onward, back, n))
    return jnp.concatenate(outs, axis=0)


def solution(mesh):
    return jax.shard_map(
        functools.partial(body, mesh.shape["row"]),
        mesh=mesh,
        in_specs=(
            P(("groups", "row"), "col"),
            P("col", "row"),
            P("col", "row"),
            P("row", "col"),
            P("col", "row"),
            P("col", "row"),
            P("row", "col"),
        ),
        out_specs=P(("groups", "row"), "col"),
        check_vma=False,
    )
```

```python
import functools

import jax
import jax.numpy as jnp
from jax import lax
from jax.experimental import pallas as pl
from jax.experimental.pallas import tpu as pltpu
from jax.sharding import PartitionSpec as P

SIDE = 128
DEPTH = 2
ITEMS = 8
AHEAD = 4
CHUNKS = 2
F32 = jnp.float32
BF16 = jnp.bfloat16


def round_up(n, unit):
    return -(-n // unit) * unit


def kept_items(mask):
    deep, wide = mask.shape
    kept = (mask != 0).astype(jnp.int32).T
    row = jnp.arange(deep)
    before = jnp.sum(jnp.where(row[None, :, None] > row[None, None, :], kept[:, None, :], 0), axis=2)
    filled = round_up(jnp.sum(kept, axis=1), DEPTH)
    column = jnp.arange(wide)
    ends = jnp.sum(jnp.where(column[:, None] >= column[None, :], filled[None, :], 0), axis=1)
    place = jnp.where(kept != 0, (ends - filled)[:, None] + before, -1)
    spots = jnp.arange(round_up(wide * round_up(deep, DEPTH), DEPTH * ITEMS))
    rows = deep + jnp.sum(
        jnp.where(place[None] == spots[:, None, None], row[None, None, :] - deep, 0), axis=(1, 2)
    )
    columns = jnp.sum((ends[None, :] <= spots[::DEPTH][:, None]).astype(jnp.int32), axis=1)
    trips = round_up(ends[-1:], DEPTH * ITEMS) // (DEPTH * ITEMS)
    return rows.astype(jnp.int32), jnp.minimum(columns, wide - 1).astype(jnp.int32), trips.astype(jnp.int32)


def block_of(i):
    return pl.ds(pl.multiple_of(i * SIDE, SIDE), SIDE)


def start_fetches(k, rows, columns, weight, fetched, sems):
    deep = weight.shape[0] // SIDE
    for t in range(ITEMS):
        item = k * ITEMS + t
        column = columns[item]
        for d in range(DEPTH):
            i = rows[item * DEPTH + d]
            i = jnp.where(i == deep, 0, i)
            pltpu.make_async_copy(
                weight.at[block_of(i), block_of(column)],
                fetched.at[block_of(item * DEPTH + d), :],
                sems.at[lax.rem(k, 2 * AHEAD)],
            ).start()


def first_fetches(rows, columns, trips, weight, fetched, sems):
    lax.fori_loop(
        0,
        jnp.minimum(AHEAD, trips[0]),
        lambda k, _: (start_fetches(k, rows, columns, weight, fetched, sems), 0)[1],
        0,
    )


def multiply(rows, columns, trips, weight, held, fetched, sems, total):
    def trip(k, _):
        @pl.when(k + AHEAD < trips[0])
        def _():
            start_fetches(k + AHEAD, rows, columns, weight, fetched, sems)

        span = ITEMS * DEPTH * SIDE
        here = fetched.at[pl.ds(pl.multiple_of(k * span, span), span), :]
        pltpu.make_async_copy(here, here, sems.at[lax.rem(k, 2 * AHEAD)]).wait()
        for t in range(ITEMS):
            item = k * ITEMS + t
            lhs = jnp.concatenate([held[:, block_of(rows[item * DEPTH + d])] for d in range(DEPTH)], axis=1)
            deep = DEPTH * SIDE
            rhs = fetched[pl.ds(pl.multiple_of(item * deep, deep), deep), :]
            total[:, block_of(columns[item])] += jnp.dot(lhs, rhs, preferred_element_type=F32)
        return 0

    lax.fori_loop(0, trips[0], trip, 0)


def scratch(rows, deep, spots):
    return [
        pltpu.VMEM((rows, deep + SIDE), BF16),
        pltpu.VMEM((spots * SIDE, SIDE), BF16),
        pltpu.SemaphoreType.DMA((2 * AHEAD,)),
    ]


SMEM = pl.BlockSpec(memory_space=pltpu.SMEM)
VMEM = pl.BlockSpec(memory_space=pltpu.VMEM)
ANY = pl.BlockSpec(memory_space=pl.ANY)


def tokens_kernel(places, rows, columns, trips, *refs):
    pieces = refs[: len(places)]
    weight, out, held, fetched, sems, piece_sems = refs[len(places) :]
    copies = [
        pltpu.make_async_copy(
            piece, held.at[pl.ds(row, piece.shape[0]), pl.ds(column, piece.shape[1])], piece_sems.at[k]
        )
        for k, (piece, (row, column)) in enumerate(zip(pieces, places))
    ]
    for copy in copies:
        copy.start()
    first_fetches(rows, columns, trips, weight, fetched, sems)
    held[:, weight.shape[0] :] = jnp.zeros((held.shape[0], SIDE), BF16)
    out[...] = jnp.zeros(out.shape, F32)
    for copy in copies:
        copy.wait()
    multiply(rows, columns, trips, weight, held, fetched, sems, out)


def tokens_product(items, pieces, places, weight):
    deep, width = weight.shape
    rows = max(row + piece.shape[0] for piece, (row, _) in zip(pieces, places))
    return pl.pallas_call(
        functools.partial(tokens_kernel, places),
        out_shape=jax.ShapeDtypeStruct((rows, width), F32),
        in_specs=[SMEM] * 3 + [ANY] * (len(pieces) + 1),
        out_specs=VMEM,
        scratch_shapes=scratch(rows, deep, items[0].shape[0]) + [pltpu.SemaphoreType.DMA((len(pieces),))],
        compiler_params=pltpu.CompilerParams(vmem_limit_bytes=40 << 20),
        cost_estimate=pl.CostEstimate(
            flops=rows * deep * width * 2, bytes_accessed=deep * width * 2, transcendentals=0
        ),
    )(*items, *pieces, weight)


SPLIT = 4


def down_kernel(far, rows, columns, trips, *refs):
    sums = refs[:4]
    down, out, on, back, held, fetched, sems, total, *parts, sum_sems = refs[4:]
    count = held.shape[0] // SPLIT

    def copies(r):
        at = pl.ds(r * count, count)
        return [pltpu.make_async_copy(sums[s].at[at], parts[s].at[at], sum_sems.at[r, s]) for s in range(4)]

    for r in range(SPLIT):
        for copy in copies(r):
            copy.start()
    first_fetches(rows, columns, trips, down, fetched, sems)
    deep = down.shape[0]
    held[:, deep:] = jnp.zeros((held.shape[0], SIDE), BF16)
    total[...] = jnp.zeros(total.shape, F32)
    for r in range(SPLIT):
        for copy in copies(r):
            copy.wait()

        def some(s, _, r=r):
            at = pl.ds(pl.multiple_of(r * count + s * 16, 16), 16)
            gate = parts[0][at, :] + parts[1][at, :]
            up = parts[2][at, :] + parts[3][at, :]
            held[at, pl.ds(0, deep)] = (gate / (1.0 + jnp.exp(-gate)) * up).astype(BF16)
            return 0

        lax.fori_loop(0, count // 16, some, 0)
    multiply(rows, columns, trips, down, held, fetched, sems, total)
    near = out.shape[0]
    half = on.shape[1]
    out[...] = total[pl.ds(0, near), :]
    on[...] = total[pl.ds(near, far), pl.ds(0, half)].astype(BF16)
    back[...] = total[pl.ds(near, far), pl.ds(half, half)].astype(BF16)


def down_product(items, sums, down, far):
    deep, width = down.shape
    rows = sums[0].shape[0]
    halves = jax.ShapeDtypeStruct((far, width // 2), BF16)
    return pl.pallas_call(
        functools.partial(down_kernel, far),
        out_shape=(jax.ShapeDtypeStruct((rows - far, width), F32), halves, halves),
        in_specs=[SMEM] * 3 + [ANY] * 5,
        out_specs=(VMEM, VMEM, VMEM),
        scratch_shapes=scratch(rows, deep, items[0].shape[0])
        + [pltpu.VMEM((rows, width), F32)]
        + [pltpu.VMEM((rows, deep), F32)] * 4
        + [pltpu.SemaphoreType.DMA((SPLIT, 4))],
        compiler_params=pltpu.CompilerParams(vmem_limit_bytes=50 << 20),
        cost_estimate=pl.CostEstimate(
            flops=rows * deep * width * 2, bytes_accessed=deep * width * 2, transcendentals=rows * deep
        ),
    )(*items, *sums, down)


def ring_of(n):
    order = list(range(n)) if n > 8 else list(range(0, n, 2)) + list(range(n - 1, 0, -2))
    onward = [(order[k], order[(k + 1) % n]) for k in range(n)]
    return onward, [(b, a) for a, b in onward]


def gather(block, onward, back, n):
    behind, ahead = [block], [block]
    for _ in range(n // 2 - 1):
        behind.append(lax.ppermute(behind[-1], "row", onward))
        ahead.append(lax.ppermute(ahead[-1], "row", back))
    half = block.shape[1] // 2
    left = lax.ppermute(behind[-1][:, :half], "row", onward)
    right = lax.ppermute(ahead[-1][:, half:], "row", back)
    return behind + ahead[1:], (left, right)


def scatter(near, on, ba, rows, onward, back, n):
    half = near.shape[1] // 2
    far = n // 2

    def block(k):
        at = -k if k <= 0 else far - 1 + k
        return near[at * rows : (at + 1) * rows]

    on = lax.ppermute(on, "row", onward)
    ba = lax.ppermute(ba, "row", back)
    for k in range(far - 1, 0, -1):
        if k == far - 1:
            on_sum = jnp.concatenate((block(k)[:, :half] + on.astype(F32), block(k)[:, half:]), axis=1)
            ba_sum = jnp.concatenate((block(-k)[:, :half], block(-k)[:, half:] + ba.astype(F32)), axis=1)
        else:
            on_sum = block(k) + on.astype(F32)
            ba_sum = block(-k) + ba.astype(F32)
        on = lax.ppermute(on_sum.astype(BF16), "row", onward)
        ba = lax.ppermute(ba_sum.astype(BF16), "row", back)
    return (block(0) + on.astype(F32) + ba.astype(F32)).astype(BF16)


def body(n, tokens, gate, up, down, gate_mask, up_mask, down_mask):
    onward, back = ring_of(n)
    swap = [(0, 1), (1, 0)]
    rows = tokens.shape[0] // CHUNKS
    half = tokens.shape[1] // 2
    gate_items, up_items, down_items = kept_items(gate_mask), kept_items(up_mask), kept_items(down_mask)

    outs = []
    for c in range(CHUNKS):
        blocks, (left, right) = gather(tokens[c * rows : (c + 1) * rows], onward, back, n)
        pieces = blocks + [left, right]
        places = [(k * rows, 0) for k in range(n - 1)] + [((n - 1) * rows, 0), ((n - 1) * rows, half)]
        gates = tokens_product(gate_items, pieces, places, gate)
        ups = tokens_product(up_items, pieces, places, up)
        sums = (gates, lax.ppermute(gates, "col", swap), ups, lax.ppermute(ups, "col", swap))
        outs.append(scatter(*down_product(down_items, sums, down, rows), rows, onward, back, n))
    return jnp.concatenate(outs, axis=0)


def solution(mesh):
    return jax.shard_map(
        functools.partial(body, mesh.shape["row"]),
        mesh=mesh,
        in_specs=(
            P(("groups", "row"), "col"),
            P("col", "row"),
            P("col", "row"),
            P("row", "col"),
            P("col", "row"),
            P("col", "row"),
            P("row", "col"),
        ),
        out_specs=P(("groups", "row"), "col"),
        check_vma=False,
    )
```

```python
import functools

import jax
import jax.numpy as jnp
from jax import lax
from jax.experimental import pallas as pl
from jax.experimental.pallas import tpu as pltpu
from jax.sharding import PartitionSpec as P

SIDE = 128
DEPTH = 2
ITEMS = 8
AHEAD = 4
SLOTS = AHEAD + 1
F32 = jnp.float32
BF16 = jnp.bfloat16


def round_up(n, unit):
    return -(-n // unit) * unit


def kept_items(mask):
    deep, wide = mask.shape
    kept = (mask != 0).astype(jnp.int32).T
    row = jnp.arange(deep)
    before = jnp.sum(jnp.where(row[None, :, None] > row[None, None, :], kept[:, None, :], 0), axis=2)
    filled = round_up(jnp.sum(kept, axis=1), DEPTH)
    column = jnp.arange(wide)
    ends = jnp.sum(jnp.where(column[:, None] >= column[None, :], filled[None, :], 0), axis=1)
    place = jnp.where(kept != 0, (ends - filled)[:, None] + before, -1)
    spots = jnp.arange(round_up(wide * round_up(deep, DEPTH), DEPTH * ITEMS))
    rows = deep + jnp.sum(
        jnp.where(place[None] == spots[:, None, None], row[None, None, :] - deep, 0), axis=(1, 2)
    )
    columns = jnp.sum((ends[None, :] <= spots[::DEPTH][:, None]).astype(jnp.int32), axis=1)
    trips = round_up(ends[-1:], DEPTH * ITEMS) // (DEPTH * ITEMS)
    return rows.astype(jnp.int32), jnp.minimum(columns, wide - 1).astype(jnp.int32), trips.astype(jnp.int32)


def block_of(i):
    return pl.ds(pl.multiple_of(i * SIDE, SIDE), SIDE)


def start_fetches(k, rows, columns, weight, fetched, sems):
    deep = weight.shape[0] // SIDE
    slot = lax.rem(k, SLOTS)
    for t in range(ITEMS):
        item = k * ITEMS + t
        column = columns[item]
        for d in range(DEPTH):
            i = rows[item * DEPTH + d]
            i = jnp.where(i == deep, 0, i)
            pltpu.make_async_copy(
                weight.at[block_of(i), block_of(column)],
                fetched.at[slot, pl.ds((t * DEPTH + d) * SIDE, SIDE), :],
                sems.at[slot],
            ).start()


def first_fetches(rows, columns, trips, weight, fetched, sems):
    lax.fori_loop(
        0,
        jnp.minimum(AHEAD, trips[0]),
        lambda k, _: (start_fetches(k, rows, columns, weight, fetched, sems), 0)[1],
        0,
    )


def multiply(rows, columns, trips, weight, held, fetched, sems, total):
    def trip(k, _):
        @pl.when(k + AHEAD < trips[0])
        def _():
            start_fetches(k + AHEAD, rows, columns, weight, fetched, sems)

        slot = lax.rem(k, SLOTS)
        pltpu.make_async_copy(fetched.at[slot], fetched.at[slot], sems.at[slot]).wait()
        for t in range(ITEMS):
            item = k * ITEMS + t
            lhs = jnp.concatenate([held[:, block_of(rows[item * DEPTH + d])] for d in range(DEPTH)], axis=1)
            deep = DEPTH * SIDE
            rhs = fetched[slot, pl.ds(t * deep, deep), :]
            total[:, block_of(columns[item])] += jnp.dot(lhs, rhs, preferred_element_type=F32)
        return 0

    lax.fori_loop(0, trips[0], trip, 0)


FETCH_SCRATCH = [pltpu.VMEM((SLOTS, ITEMS * DEPTH * SIDE, SIDE), BF16), pltpu.SemaphoreType.DMA((SLOTS,))]


SMEM = pl.BlockSpec(memory_space=pltpu.SMEM)
VMEM = pl.BlockSpec(memory_space=pltpu.VMEM)
HBM = pl.BlockSpec(memory_space=pltpu.HBM)


def tokens_kernel(places, *refs):
    lists, refs = refs[:6], refs[6:]
    pieces = refs[: len(places)]
    gate, up, out, held, *rest = refs[len(places) :]
    piece_sems = rest[-1]
    jobs = [(*lists[3 * w : 3 * w + 3], weight, *rest[2 * w : 2 * w + 2]) for w, weight in enumerate((gate, up))]
    copies = [
        pltpu.make_async_copy(
            piece, held.at[pl.ds(row, piece.shape[0]), pl.ds(column, piece.shape[1])], piece_sems.at[k]
        )
        for k, (piece, (row, column)) in enumerate(zip(pieces, places))
    ]
    for copy in copies:
        copy.start()
    for job in jobs:
        first_fetches(*job)
    held[:, gate.shape[0] :] = jnp.zeros((held.shape[0], SIDE), BF16)
    out[...] = jnp.zeros(out.shape, F32)
    for copy in copies:
        copy.wait()
    width = gate.shape[1]
    for w, (rows, columns, trips, weight, fetched, sems) in enumerate(jobs):
        multiply(rows, columns, trips, weight, held, fetched, sems, out.at[:, pl.ds(w * width, width)])


def tokens_product(gate_items, up_items, pieces, places, gate, up):
    deep, width = gate.shape
    rows = max(row + piece.shape[0] for piece, (row, _) in zip(pieces, places))
    return pl.pallas_call(
        functools.partial(tokens_kernel, places),
        out_shape=jax.ShapeDtypeStruct((rows, 2 * width), F32),
        in_specs=[SMEM] * 6 + [VMEM] * len(pieces) + [HBM] * 2,
        out_specs=VMEM,
        scratch_shapes=[
            pltpu.VMEM((rows, deep + SIDE), BF16),
            *FETCH_SCRATCH,
            *FETCH_SCRATCH,
            pltpu.SemaphoreType.DMA((len(pieces),)),
        ],
        compiler_params=pltpu.CompilerParams(vmem_limit_bytes=20 << 20),
        cost_estimate=pl.CostEstimate(
            flops=rows * deep * width * 4, bytes_accessed=deep * width * 4, transcendentals=0
        ),
    )(*gate_items, *up_items, *pieces, gate, up)


def down_kernel(groups, opposite, rows, columns, trips, *refs):
    sums, refs = refs[: 2 * groups], refs[2 * groups :]
    down, refs = refs[0], refs[1:]
    if opposite:
        on, back, total, held, fetched, sems = refs
    else:
        total, held, fetched, sems = refs
    first_fetches(rows, columns, trips, down, fetched, sems)
    deep = down.shape[0]
    held[:, deep:] = jnp.zeros((held.shape[0], SIDE), BF16)
    total[...] = jnp.zeros(total.shape, F32)
    at = 0
    for g in range(groups):
        mine, other = sums[2 * g : 2 * g + 2]

        def some(s, _, at=at, mine=mine, other=other):
            here = pl.ds(pl.multiple_of(s * 16, 16), 16)
            value = mine[here, :] + other[here, :]
            silu = value[:, :deep] / (1.0 + jnp.exp(-value[:, :deep]))
            held[pl.ds(pl.multiple_of(at + s * 16, 16), 16), pl.ds(0, deep)] = (silu * value[:, deep:]).astype(BF16)
            return 0

        lax.fori_loop(0, mine.shape[0] // 16, some, 0)
        at += mine.shape[0]
    multiply(rows, columns, trips, down, held, fetched, sems, total)
    if opposite:
        half = on.shape[1]
        on[...] = total[:, pl.ds(0, half)].astype(BF16)
        back[...] = total[:, pl.ds(half, half)].astype(BF16)


def down_product(items, sums, down, opposite):
    deep, width = down.shape
    groups = len(sums)
    rows = sum(mine.shape[0] for mine, _ in sums)
    whole = pltpu.VMEM((rows, width), F32)
    half = jax.ShapeDtypeStruct((rows, width // 2), BF16)
    return pl.pallas_call(
        functools.partial(down_kernel, groups, opposite),
        out_shape=(half, half) if opposite else jax.ShapeDtypeStruct((rows, width), F32),
        in_specs=[SMEM] * 3 + [VMEM] * (2 * groups) + [HBM],
        out_specs=(VMEM, VMEM) if opposite else VMEM,
        scratch_shapes=([whole] if opposite else [])
        + [pltpu.VMEM((rows, deep + SIDE), BF16)]
        + FETCH_SCRATCH,
        compiler_params=pltpu.CompilerParams(vmem_limit_bytes=20 << 20),
        cost_estimate=pl.CostEstimate(
            flops=rows * deep * width * 2, bytes_accessed=deep * width * 2, transcendentals=rows * deep
        ),
    )(*items, *(part for pair in sums for part in pair), down)


def ring_of(n):
    order = list(range(n)) if n > 8 else list(range(0, n, 2)) + list(range(n - 1, 0, -2))
    onward = [(order[k], order[(k + 1) % n]) for k in range(n)]
    return onward, [(b, a) for a, b in onward]


def tie(values, *before):
    return lax.optimization_barrier((values, before))[0]


def scatter(parts, onward, back, n):
    far = n // 2
    on, ba = parts[far]
    half = on.shape[1]
    for k in range(far, 0, -1):
        on, ba = lax.ppermute(on, "row", onward).astype(F32), lax.ppermute(ba, "row", back).astype(F32)
        if k == 1:
            return (parts[0][0] + on + ba).astype(BF16)
        behind, ahead = parts[k - 1]
        if k == far:
            on = jnp.concatenate((ahead[:, :half] + on, ahead[:, half:]), axis=1)
            ba = jnp.concatenate((behind[:, :half], behind[:, half:] + ba), axis=1)
        else:
            on, ba = ahead + on, behind + ba
        on, ba = tie((on.astype(BF16), ba.astype(BF16)))


def body(n, tokens, gate, up, down, gate_mask, up_mask, down_mask):
    onward, back = ring_of(n)
    swap = [(0, 1), (1, 0)]
    far = n // 2
    half = tokens.shape[1] // 2
    gate_items, up_items, down_items = kept_items(gate_mask), kept_items(up_mask), kept_items(down_mask)
    rows = tokens.shape[0]
    def product(group):
        pieces, places = [], []
        at = 0
        for k in group:
            for piece in steps[k]:
                pieces.append(piece)
                places.append((at, 0))
                at += rows
        if group[-1] == far:
            places[-2:] = [(at - 2 * rows, 0), (at - 2 * rows, half)]
        mine = tokens_product(gate_items, up_items, pieces, places, gate, up)
        return mine, lax.ppermute(mine, "col", swap)

    gate, up, down = (pltpu.with_memory_space_constraint(w, pltpu.HBM) for w in (gate, up, down))
    behind = ahead = tokens
    steps = [(tokens,)]
    sums = []
    for k in range(1, far + 1):
        if k > 2:
            sums.append(product((0, 1) if k == 3 else (k - 2,)))
            behind, ahead = tie((behind, ahead), sums[-1][0])
        if k == far:
            behind, ahead = behind[:, :half], ahead[:, half:]
        behind, ahead = lax.ppermute(behind, "row", onward), lax.ppermute(ahead, "row", back)
        steps.append((behind, ahead))
    sums += [product((far - 1,)), product((far,))]
    parts = [None] * (far + 1)
    parts[far] = down_product(down_items, sums[-1:], down, True)
    late = down_product(down_items, sums[-2:-1], down, False)
    early = down_product(down_items, sums[:-2], down, False)
    parts[0] = (early[:rows],)
    for k in range(1, far):
        source, at = (late, 0) if k == far - 1 else (early, (2 * k - 1) * rows)
        parts[k] = (source[at : at + rows], source[at + rows : at + 2 * rows])
    return scatter(parts, onward, back, n)


def solution(mesh):
    return jax.shard_map(
        functools.partial(body, mesh.shape["row"]),
        mesh=mesh,
        in_specs=(
            P(("groups", "row"), "col"),
            P("col", "row"),
            P("col", "row"),
            P("row", "col"),
            P("col", "row"),
            P("col", "row"),
            P("row", "col"),
        ),
        out_specs=P(("groups", "row"), "col"),
        check_vma=False,
    )
```

```python
import functools

import jax
import jax.numpy as jnp
from jax import lax
from jax.experimental import pallas as pl
from jax.experimental.pallas import tpu as pltpu
from jax.sharding import PartitionSpec as P

SIDE = 128
DEPTH = 2
ITEMS = 8
AHEAD = 8
SLOTS = AHEAD + 1
F32 = jnp.float32
BF16 = jnp.bfloat16


def round_up(n, unit):
    return -(-n // unit) * unit


def kept_items(mask):
    deep, wide = mask.shape
    kept = (mask != 0).astype(jnp.int32).T
    row = jnp.arange(deep)
    before = jnp.sum(jnp.where(row[None, :, None] > row[None, None, :], kept[:, None, :], 0), axis=2)
    filled = round_up(jnp.sum(kept, axis=1), DEPTH)
    column = jnp.arange(wide)
    ends = jnp.sum(jnp.where(column[:, None] >= column[None, :], filled[None, :], 0), axis=1)
    place = jnp.where(kept != 0, (ends - filled)[:, None] + before, -1)
    spots = jnp.arange(round_up(wide * round_up(deep, DEPTH), DEPTH * ITEMS))
    rows = deep + jnp.sum(
        jnp.where(place[None] == spots[:, None, None], row[None, None, :] - deep, 0), axis=(1, 2)
    )
    items = jnp.arange(spots.shape[0] // DEPTH + 1)
    columns = jnp.sum((ends[None, :] <= items[:, None] * DEPTH).astype(jnp.int32), axis=1)
    trips = round_up(jnp.max(ends[None, :] + items[:, None], axis=1) - items, DEPTH * ITEMS) // (DEPTH * ITEMS)
    columns = jnp.where(items == items.shape[0] - 1, trips, jnp.minimum(columns, wide - 1))
    return rows.astype(jnp.int32), columns.astype(jnp.int32)


def trips_of(columns):
    return columns[columns.shape[0] - 1]


def block_of(i):
    return pl.ds(pl.multiple_of(i * SIDE, SIDE), SIDE)


def start_fetches(k, rows, columns, weight, fetched, sems):
    deep = weight.shape[0] // SIDE
    slot = lax.rem(k, SLOTS)
    for t in range(ITEMS):
        item = k * ITEMS + t
        column = columns[item]
        for d in range(DEPTH):
            i = rows[item * DEPTH + d]
            i = jnp.where(i == deep, 0, i)
            pltpu.make_async_copy(
                weight.at[block_of(i), block_of(column)],
                fetched.at[slot, pl.ds((t * DEPTH + d) * SIDE, SIDE), :],
                sems.at[slot],
            ).start()


def first_fetches(rows, columns, weight, fetched, sems):
    lax.fori_loop(
        0,
        jnp.minimum(AHEAD, trips_of(columns)),
        lambda k, _: (start_fetches(k, rows, columns, weight, fetched, sems), 0)[1],
        0,
    )


def multiply_trip(k, rows, columns, held, blocks, total):
    deep = DEPTH * SIDE
    for t in range(ITEMS):
        item = k * ITEMS + t
        lhs = jnp.concatenate([held[:, block_of(rows[item * DEPTH + d])] for d in range(DEPTH)], axis=1)
        rhs = blocks[pl.ds(t * deep, deep), :]
        total[:, block_of(columns[item])] += jnp.dot(lhs, rhs, preferred_element_type=F32)


def multiply(rows, columns, weight, held, fetched, sems, total):
    def trip(k, _, more):
        slot = lax.rem(k, SLOTS)
        pltpu.make_async_copy(fetched.at[slot], fetched.at[slot], sems.at[slot]).wait()
        multiply_trip(k, rows, columns, held, fetched.at[slot], total)
        if more:
            start_fetches(k + AHEAD, rows, columns, weight, fetched, sems)
        return 0

    trips = trips_of(columns)
    last = jnp.maximum(trips - AHEAD, 0)
    lax.fori_loop(0, last, functools.partial(trip, more=True), 0)
    lax.fori_loop(last, trips, functools.partial(trip, more=False), 0)


FETCH_SCRATCH = [pltpu.VMEM((SLOTS, ITEMS * DEPTH * SIDE, SIDE), BF16), pltpu.SemaphoreType.DMA((SLOTS,))]


SMEM = pl.BlockSpec(memory_space=pltpu.SMEM)
VMEM = pl.BlockSpec(memory_space=pltpu.VMEM)
HBM = pl.BlockSpec(memory_space=pltpu.HBM)


def pack_kernel(*refs):
    lists, (gate, up, gate_packed, up_packed, sems) = refs[:4], refs[4:]
    jobs = [(*lists[2 * w : 2 * w + 2], *ends) for w, ends in enumerate(((gate, gate_packed), (up, up_packed)))]

    def start(k, _, w, rows, columns, weight, packed):
        deep = weight.shape[0] // SIDE
        for t in range(ITEMS * DEPTH):
            place = k * ITEMS * DEPTH + t
            i = rows[place]
            pltpu.make_async_copy(
                weight.at[block_of(jnp.where(i == deep, 0, i)), block_of(columns[k * ITEMS + t // DEPTH])],
                packed.at[block_of(place), :],
                sems.at[w],
            ).start()
        return 0

    def wait(k, _, w, packed):
        span = ITEMS * DEPTH * SIDE
        here = packed.at[pl.ds(pl.multiple_of(k * span, span), span), :]
        pltpu.make_async_copy(here, here, sems.at[w]).wait()
        return 0

    for w, (rows, columns, weight, packed) in enumerate(jobs):
        lax.fori_loop(
            0, trips_of(columns), functools.partial(start, w=w, rows=rows, columns=columns, weight=weight, packed=packed), 0
        )
    for w, (_, columns, _, packed) in enumerate(jobs):
        lax.fori_loop(0, trips_of(columns), functools.partial(wait, w=w, packed=packed), 0)


def pack(gate_items, up_items, gate, up):
    return pl.pallas_call(
        pack_kernel,
        out_shape=[jax.ShapeDtypeStruct((items[0].shape[0] * SIDE, SIDE), BF16) for items in (gate_items, up_items)],
        in_specs=[SMEM] * 4 + [HBM] * 2,
        out_specs=[VMEM] * 2,
        scratch_shapes=[pltpu.SemaphoreType.DMA((2,))],
        compiler_params=pltpu.CompilerParams(vmem_limit_bytes=1 << 20),
        cost_estimate=pl.CostEstimate(flops=0, bytes_accessed=2 * gate.size, transcendentals=0),
    )(*gate_items, *up_items, gate, up)


def tokens_kernel(places, *refs):
    lists, refs = refs[:4], refs[4:]
    pieces = refs[: len(places)]
    gate, up, out, held, sems = refs[len(places) :]
    deep = held.shape[1] - SIDE
    width = out.shape[1] // 2
    copies = [
        pltpu.make_async_copy(piece, held.at[pl.ds(row, piece.shape[0]), pl.ds(column, piece.shape[1])], sems.at[k])
        for k, (piece, (row, column)) in enumerate(zip(pieces, places))
    ]
    for copy in copies:
        copy.start()
    held[:, deep:] = jnp.zeros((held.shape[0], SIDE), BF16)
    out[...] = jnp.zeros(out.shape, F32)
    for copy in copies:
        copy.wait()
    span = ITEMS * DEPTH * SIDE
    for w, packed in enumerate((gate, up)):
        rows, columns = lists[2 * w : 2 * w + 2]

        def trip(k, _, rows=rows, columns=columns, packed=packed, w=w):
            blocks = packed.at[pl.ds(pl.multiple_of(k * span, span), span), :]
            multiply_trip(k, rows, columns, held, blocks, out.at[:, pl.ds(w * width, width)])
            return 0

        lax.fori_loop(0, trips_of(columns), trip, 0)


def tokens_product(gate_items, up_items, pieces, places, gate, up, deep, width):
    rows = max(row + piece.shape[0] for piece, (row, _) in zip(pieces, places))
    return pl.pallas_call(
        functools.partial(tokens_kernel, places),
        out_shape=jax.ShapeDtypeStruct((rows, 2 * width), F32),
        in_specs=[SMEM] * 4 + [VMEM] * (len(pieces) + 2),
        out_specs=VMEM,
        scratch_shapes=[pltpu.VMEM((rows, deep + SIDE), BF16), pltpu.SemaphoreType.DMA((len(pieces),))],
        compiler_params=pltpu.CompilerParams(vmem_limit_bytes=6 << 20),
        cost_estimate=pl.CostEstimate(
            flops=16 * rows * deep * width, bytes_accessed=16 * deep * width, transcendentals=0
        ),
    )(*gate_items, *up_items, *pieces, gate, up)


def down_kernel(groups, opposite, rows, columns, *refs):
    sums, refs = refs[: 2 * groups], refs[2 * groups :]
    down, refs = refs[0], refs[1:]
    if opposite:
        on, back, total, held, fetched, sems = refs
    else:
        total, held, fetched, sems = refs
    first_fetches(rows, columns, down, fetched, sems)
    deep = down.shape[0]
    held[:, deep:] = jnp.zeros((held.shape[0], SIDE), BF16)
    total[...] = jnp.zeros(total.shape, F32)
    at = 0
    for g in range(groups):
        mine, other = sums[2 * g : 2 * g + 2]

        def some(s, _, at=at, mine=mine, other=other):
            here = pl.ds(pl.multiple_of(s * 16, 16), 16)
            value = mine[here, :] + other[here, :]
            silu = value[:, :deep] / (1.0 + jnp.exp(-value[:, :deep]))
            held[pl.ds(pl.multiple_of(at + s * 16, 16), 16), pl.ds(0, deep)] = (silu * value[:, deep:]).astype(BF16)
            return 0

        lax.fori_loop(0, mine.shape[0] // 16, some, 0)
        at += mine.shape[0]
    multiply(rows, columns, down, held, fetched, sems, total)
    if opposite:
        half = on.shape[1]
        on[...] = total[:, pl.ds(0, half)].astype(BF16)
        back[...] = total[:, pl.ds(half, half)].astype(BF16)


def down_product(items, sums, down, opposite):
    deep, width = down.shape
    groups = len(sums)
    rows = sum(mine.shape[0] for mine, _ in sums)
    whole = pltpu.VMEM((rows, width), F32)
    half = jax.ShapeDtypeStruct((rows, width // 2), BF16)
    return pl.pallas_call(
        functools.partial(down_kernel, groups, opposite),
        out_shape=(half, half) if opposite else jax.ShapeDtypeStruct((rows, width), F32),
        in_specs=[SMEM] * 2 + [VMEM] * (2 * groups) + [HBM],
        out_specs=(VMEM, VMEM) if opposite else VMEM,
        scratch_shapes=([whole] if opposite else [])
        + [pltpu.VMEM((rows, deep + SIDE), BF16)]
        + FETCH_SCRATCH,
        compiler_params=pltpu.CompilerParams(vmem_limit_bytes=14 << 20),
        cost_estimate=pl.CostEstimate(
            flops=rows * deep * width * 2, bytes_accessed=deep * width * 2, transcendentals=rows * deep
        ),
    )(*items, *(part for pair in sums for part in pair), down)


def ring_of(n):
    order = list(range(n)) if n > 8 else list(range(0, n, 2)) + list(range(n - 1, 0, -2))
    onward = [(order[k], order[(k + 1) % n]) for k in range(n)]
    return onward, [(b, a) for a, b in onward]


def tie(values, *before):
    return lax.optimization_barrier((values, before))[0]


def scatter(parts, onward, back, n):
    far = n // 2
    on, ba = parts[far]
    half = on.shape[1]
    for k in range(far, 0, -1):
        on, ba = lax.ppermute(on, "row", onward).astype(F32), lax.ppermute(ba, "row", back).astype(F32)
        if k == 1:
            return (parts[0][0] + on + ba).astype(BF16)
        behind, ahead = parts[k - 1]
        if k == far:
            on = jnp.concatenate((ahead[:, :half] + on, ahead[:, half:]), axis=1)
            ba = jnp.concatenate((behind[:, :half], behind[:, half:] + ba), axis=1)
        else:
            on, ba = ahead + on, behind + ba
        on, ba = tie((on.astype(BF16), ba.astype(BF16)))


def body(n, tokens, gate, up, down, gate_mask, up_mask, down_mask):
    onward, back = ring_of(n)
    swap = [(0, 1), (1, 0)]
    far = n // 2
    half = tokens.shape[1] // 2
    gate_items, up_items, down_items = kept_items(gate_mask), kept_items(up_mask), kept_items(down_mask)
    rows = tokens.shape[0]
    def product(group):
        pieces, places = [], []
        at = 0
        for k in group:
            for piece in steps[k]:
                pieces.append(piece)
                places.append((at, 0))
                at += rows
        if group[-1] == far:
            places[-2:] = [(at - 2 * rows, 0), (at - 2 * rows, half)]
        mine = tokens_product(gate_items, up_items, pieces, places, *packed, *gate.shape)
        return mine, lax.ppermute(mine, "col", swap)

    gate, up, down = (pltpu.with_memory_space_constraint(w, pltpu.HBM) for w in (gate, up, down))
    packed = pack(gate_items, up_items, gate, up)
    behind = ahead = tokens
    steps = [(tokens,)]
    sums = []
    for k in range(1, far + 1):
        if k > 2:
            sums.append(product((0, 1) if k == 3 else (k - 2,)))
            behind, ahead = tie((behind, ahead), sums[-1][0])
        if k == far:
            behind, ahead = behind[:, :half], ahead[:, half:]
        behind, ahead = lax.ppermute(behind, "row", onward), lax.ppermute(ahead, "row", back)
        steps.append((behind, ahead))
    sums += [product((far - 1,)), product((far,))]
    parts = [None] * (far + 1)
    parts[far] = down_product(down_items, sums[-1:], down, True)
    late = down_product(down_items, sums[-2:-1], down, False)
    early = down_product(down_items, sums[:-2], down, False)
    parts[0] = (early[:rows],)
    for k in range(1, far):
        source, at = (late, 0) if k == far - 1 else (early, (2 * k - 1) * rows)
        parts[k] = (source[at : at + rows], source[at + rows : at + 2 * rows])
    return scatter(parts, onward, back, n)


def solution(mesh):
    return jax.shard_map(
        functools.partial(body, mesh.shape["row"]),
        mesh=mesh,
        in_specs=(
            P(("groups", "row"), "col"),
            P("col", "row"),
            P("col", "row"),
            P("row", "col"),
            P("col", "row"),
            P("col", "row"),
            P("row", "col"),
        ),
        out_specs=P(("groups", "row"), "col"),
        check_vma=False,
    )
```

```python
import functools

import jax
import jax.numpy as jnp
from jax import lax
from jax.experimental import pallas as pl
from jax.experimental.pallas import tpu as pltpu
from jax.sharding import PartitionSpec as P

SIDE = 128
DEPTH = 2
ITEMS = 8
AHEAD = 8
SLOTS = AHEAD + 1
F32 = jnp.float32
BF16 = jnp.bfloat16


def round_up(n, unit):
    return -(-n // unit) * unit


def kept_items(mask):
    deep, wide = mask.shape
    kept = (mask != 0).astype(jnp.int32).T
    row = jnp.arange(deep)
    before = jnp.sum(jnp.where(row[None, :, None] > row[None, None, :], kept[:, None, :], 0), axis=2)
    filled = round_up(jnp.sum(kept, axis=1), DEPTH)
    column = jnp.arange(wide)
    ends = jnp.sum(jnp.where(column[:, None] >= column[None, :], filled[None, :], 0), axis=1)
    place = jnp.where(kept != 0, (ends - filled)[:, None] + before, -1)
    spots = jnp.arange(round_up(wide * round_up(deep, DEPTH), DEPTH * ITEMS))
    rows = deep + jnp.sum(
        jnp.where(place[None] == spots[:, None, None], row[None, None, :] - deep, 0), axis=(1, 2)
    )
    items = jnp.arange(spots.shape[0] // DEPTH + 1)
    columns = jnp.sum((ends[None, :] <= items[:, None] * DEPTH).astype(jnp.int32), axis=1)
    trips = round_up(jnp.max(ends[None, :] + items[:, None], axis=1) - items, DEPTH * ITEMS) // (DEPTH * ITEMS)
    columns = jnp.where(items == items.shape[0] - 1, trips, jnp.minimum(columns, wide - 1))
    return rows.astype(jnp.int32), columns.astype(jnp.int32)


def trips_of(columns):
    return columns[columns.shape[0] - 1]


def block_of(i):
    return pl.ds(pl.multiple_of(i * SIDE, SIDE), SIDE)


def start_fetches(k, rows, columns, weight, fetched, sems):
    deep = weight.shape[0] // SIDE
    slot = lax.rem(k, SLOTS)
    for t in range(ITEMS):
        item = k * ITEMS + t
        column = columns[item]
        for d in range(DEPTH):
            i = rows[item * DEPTH + d]
            i = jnp.where(i == deep, 0, i)
            pltpu.make_async_copy(
                weight.at[block_of(i), block_of(column)],
                fetched.at[slot, pl.ds((t * DEPTH + d) * SIDE, SIDE), :],
                sems.at[slot],
            ).start()


def first_fetches(rows, columns, weight, fetched, sems):
    lax.fori_loop(
        0,
        jnp.minimum(AHEAD, trips_of(columns)),
        lambda k, _: (start_fetches(k, rows, columns, weight, fetched, sems), 0)[1],
        0,
    )


def multiply_trip(k, rows, columns, held, blocks, total):
    deep = DEPTH * SIDE
    for t in range(ITEMS):
        item = k * ITEMS + t
        lhs = jnp.concatenate([held[:, block_of(rows[item * DEPTH + d])] for d in range(DEPTH)], axis=1)
        rhs = blocks[pl.ds(t * deep, deep), :]
        total[:, block_of(columns[item])] += jnp.dot(lhs, rhs, preferred_element_type=F32)


def multiply(rows, columns, weight, held, fetched, sems, total):
    def trip(k, _, more):
        slot = lax.rem(k, SLOTS)
        pltpu.make_async_copy(fetched.at[slot], fetched.at[slot], sems.at[slot]).wait()
        multiply_trip(k, rows, columns, held, fetched.at[slot], total)
        if more:
            start_fetches(k + AHEAD, rows, columns, weight, fetched, sems)
        return 0

    trips = trips_of(columns)
    last = jnp.maximum(trips - AHEAD, 0)
    lax.fori_loop(0, last, functools.partial(trip, more=True), 0)
    lax.fori_loop(last, trips, functools.partial(trip, more=False), 0)


FETCH_SCRATCH = [pltpu.VMEM((SLOTS, ITEMS * DEPTH * SIDE, SIDE), BF16), pltpu.SemaphoreType.DMA((SLOTS,))]


SMEM = pl.BlockSpec(memory_space=pltpu.SMEM)
VMEM = pl.BlockSpec(memory_space=pltpu.VMEM)
HBM = pl.BlockSpec(memory_space=pltpu.HBM)


def pack_kernel(*refs):
    lists, (gate, up, gate_packed, up_packed, sems) = refs[:4], refs[4:]
    jobs = [(*lists[2 * w : 2 * w + 2], *ends) for w, ends in enumerate(((gate, gate_packed), (up, up_packed)))]

    def start(k, _, w, rows, columns, weight, packed):
        deep = weight.shape[0] // SIDE
        for t in range(ITEMS * DEPTH):
            place = k * ITEMS * DEPTH + t
            i = rows[place]
            pltpu.make_async_copy(
                weight.at[block_of(jnp.where(i == deep, 0, i)), block_of(columns[k * ITEMS + t // DEPTH])],
                packed.at[block_of(place), :],
                sems.at[w],
            ).start()
        return 0

    def wait(k, _, w, packed):
        span = ITEMS * DEPTH * SIDE
        here = packed.at[pl.ds(pl.multiple_of(k * span, span), span), :]
        pltpu.make_async_copy(here, here, sems.at[w]).wait()
        return 0

    for w, (rows, columns, weight, packed) in enumerate(jobs):
        lax.fori_loop(
            0, trips_of(columns), functools.partial(start, w=w, rows=rows, columns=columns, weight=weight, packed=packed), 0
        )
    for w, (_, columns, _, packed) in enumerate(jobs):
        lax.fori_loop(0, trips_of(columns), functools.partial(wait, w=w, packed=packed), 0)


def pack(gate_items, up_items, gate, up):
    return pl.pallas_call(
        pack_kernel,
        out_shape=[jax.ShapeDtypeStruct((items[0].shape[0] * SIDE, SIDE), BF16) for items in (gate_items, up_items)],
        in_specs=[SMEM] * 4 + [HBM] * 2,
        out_specs=[VMEM] * 2,
        scratch_shapes=[pltpu.SemaphoreType.DMA((2,))],
        compiler_params=pltpu.CompilerParams(vmem_limit_bytes=1 << 20),
        cost_estimate=pl.CostEstimate(flops=0, bytes_accessed=2 * gate.size, transcendentals=0),
    )(*gate_items, *up_items, gate, up)


def tokens_kernel(places, *refs):
    lists, refs = refs[:4], refs[4:]
    pieces = refs[: len(places)]
    gate, up, out, held, sems = refs[len(places) :]
    deep = held.shape[1] - SIDE
    width = out.shape[1] // 2
    copies = [
        pltpu.make_async_copy(piece, held.at[pl.ds(row, piece.shape[0]), pl.ds(column, piece.shape[1])], sems.at[k])
        for k, (piece, (row, column)) in enumerate(zip(pieces, places))
    ]
    for copy in copies:
        copy.start()
    held[:, deep:] = jnp.zeros((held.shape[0], SIDE), BF16)
    out[...] = jnp.zeros(out.shape, F32)
    for copy in copies:
        copy.wait()
    span = ITEMS * DEPTH * SIDE
    for w, packed in enumerate((gate, up)):
        rows, columns = lists[2 * w : 2 * w + 2]

        def trip(k, _, rows=rows, columns=columns, packed=packed, w=w):
            blocks = packed.at[pl.ds(pl.multiple_of(k * span, span), span), :]
            multiply_trip(k, rows, columns, held, blocks, out.at[:, pl.ds(w * width, width)])
            return 0

        lax.fori_loop(0, trips_of(columns), trip, 0)


def tokens_product(gate_items, up_items, pieces, places, gate, up, deep, width):
    rows = max(row + piece.shape[0] for piece, (row, _) in zip(pieces, places))
    return pl.pallas_call(
        functools.partial(tokens_kernel, places),
        out_shape=jax.ShapeDtypeStruct((rows, 2 * width), F32),
        in_specs=[SMEM] * 4 + [VMEM] * (len(pieces) + 2),
        out_specs=VMEM,
        scratch_shapes=[pltpu.VMEM((rows, deep + SIDE), BF16), pltpu.SemaphoreType.DMA((len(pieces),))],
        compiler_params=pltpu.CompilerParams(vmem_limit_bytes=6 << 20),
        cost_estimate=pl.CostEstimate(
            flops=16 * rows * deep * width, bytes_accessed=16 * deep * width, transcendentals=0
        ),
    )(*gate_items, *up_items, *pieces, gate, up)


def down_kernel(groups, opposite, rows, columns, *refs):
    sums, refs = refs[: 2 * groups], refs[2 * groups :]
    down, refs = refs[0], refs[1:]
    if opposite:
        on, back, total, held, fetched, sems = refs
    else:
        total, held, fetched, sems = refs
    first_fetches(rows, columns, down, fetched, sems)
    deep = down.shape[0]
    held[:, deep:] = jnp.zeros((held.shape[0], SIDE), BF16)
    total[...] = jnp.zeros(total.shape, F32)
    at = 0
    for g in range(groups):
        mine, other = sums[2 * g : 2 * g + 2]

        def some(s, _, at=at, mine=mine, other=other):
            here = pl.ds(pl.multiple_of(s * 16, 16), 16)
            value = mine[here, :] + other[here, :]
            silu = value[:, :deep] / (1.0 + jnp.exp(-value[:, :deep]))
            held[pl.ds(pl.multiple_of(at + s * 16, 16), 16), pl.ds(0, deep)] = (silu * value[:, deep:]).astype(BF16)
            return 0

        lax.fori_loop(0, mine.shape[0] // 16, some, 0)
        at += mine.shape[0]
    multiply(rows, columns, down, held, fetched, sems, total)
    if opposite:
        half = on.shape[1]
        on[...] = total[:, pl.ds(0, half)].astype(BF16)
        back[...] = total[:, pl.ds(half, half)].astype(BF16)


def down_product(items, sums, down, opposite):
    deep, width = down.shape
    groups = len(sums)
    rows = sum(mine.shape[0] for mine, _ in sums)
    whole = pltpu.VMEM((rows, width), F32)
    half = jax.ShapeDtypeStruct((rows, width // 2), BF16)
    return pl.pallas_call(
        functools.partial(down_kernel, groups, opposite),
        out_shape=(half, half) if opposite else jax.ShapeDtypeStruct((rows, width), F32),
        in_specs=[SMEM] * 2 + [VMEM] * (2 * groups) + [HBM],
        out_specs=(VMEM, VMEM) if opposite else VMEM,
        scratch_shapes=([whole] if opposite else [])
        + [pltpu.VMEM((rows, deep + SIDE), BF16)]
        + FETCH_SCRATCH,
        compiler_params=pltpu.CompilerParams(vmem_limit_bytes=14 << 20),
        cost_estimate=pl.CostEstimate(
            flops=rows * deep * width * 2, bytes_accessed=deep * width * 2, transcendentals=rows * deep
        ),
    )(*items, *(part for pair in sums for part in pair), down)


def ring_of(n):
    order = list(range(n)) if n > 8 else list(range(0, n, 2)) + list(range(n - 1, 0, -2))
    onward = [(order[k], order[(k + 1) % n]) for k in range(n)]
    return onward, [(b, a) for a, b in onward]


def tie(values, *before):
    return lax.optimization_barrier((values, before))[0]


STREAMS = 2


def scatter(opposite, late, onward, back, n):
    far = n // 2
    few = opposite[0].shape[0] // STREAMS
    half = opposite[0].shape[1]
    cut = [slice(s * few, (s + 1) * few) for s in range(STREAMS)]
    sent = [[block[rows] for block in opposite] for rows in cut]
    last = None
    for k in range(far - 1, -1, -1):
        blocks = late(k, last)
        for s, rows in enumerate(cut):
            on, ba = (lax.ppermute(block, "row", way) for block, way in zip(sent[s], (onward, back)))
            if last is not None:
                on, ba = tie((on, ba), last)
            on, ba = on.astype(F32), ba.astype(F32)
            if k == 0:
                last = sent[s] = ((blocks[0][rows] + on + ba).astype(BF16),)
                continue
            behind, ahead = (block[rows] for block in blocks)
            if k == far - 1:
                on = jnp.concatenate((ahead[:, :half] + on, ahead[:, half:]), axis=1)
                ba = jnp.concatenate((behind[:, :half], behind[:, half:] + ba), axis=1)
            else:
                on, ba = ahead + on, behind + ba
            last = sent[s] = tie((on.astype(BF16), ba.astype(BF16)))
    return jnp.concatenate([block for (block,) in sent], axis=0)


def body(n, tokens, gate, up, down, gate_mask, up_mask, down_mask):
    onward, back = ring_of(n)
    swap = [(0, 1), (1, 0)]
    far = n // 2
    half = tokens.shape[1] // 2
    gate_items, up_items, down_items = kept_items(gate_mask), kept_items(up_mask), kept_items(down_mask)
    rows = tokens.shape[0]
    def product(group):
        pieces, places = [], []
        at = 0
        for k in group:
            for piece in steps[k]:
                pieces.append(piece)
                places.append((at, 0))
                at += rows
        if group[-1] == far:
            places[-2:] = [(at - 2 * rows, 0), (at - 2 * rows, half)]
        mine = tokens_product(gate_items, up_items, pieces, places, *packed, *gate.shape)
        return mine, lax.ppermute(mine, "col", swap)

    gate, up, down = (pltpu.with_memory_space_constraint(w, pltpu.HBM) for w in (gate, up, down))
    packed = pack(gate_items, up_items, gate, up)
    behind = ahead = tokens
    steps = [(tokens,)]
    sums = []
    for k in range(1, far + 1):
        if k > 2:
            sums.append(product((0, 1) if k == 3 else (k - 2,)))
            behind, ahead = tie((behind, ahead), sums[-1][0])
        if k == far:
            behind, ahead = behind[:, :half], ahead[:, half:]
        behind, ahead = lax.ppermute(behind, "row", onward), lax.ppermute(ahead, "row", back)
        steps.append((behind, ahead))
    sums += [product((far - 1,)), product((far,))]
    near = {}

    def late(k, sent):
        if k not in near:
            group = sums[max(k - 1, 0)]
            parts = down_product(down_items, [group if sent is None else tie(group, sent)], down, False)
            for i, block in enumerate(((0,), (1, 2)) if k < 2 else ((0, 1),)):
                near[i if k < 2 else k] = [parts[j * rows : (j + 1) * rows] for j in block]
        return near[k]

    opposite = tie(sums[-1], *(other for _, other in sums[:-2]))
    return scatter(down_product(down_items, [opposite], down, True), late, onward, back, n)


def solution(mesh):
    return jax.shard_map(
        functools.partial(body, mesh.shape["row"]),
        mesh=mesh,
        in_specs=(
            P(("groups", "row"), "col"),
            P("col", "row"),
            P("col", "row"),
            P("row", "col"),
            P("col", "row"),
            P("col", "row"),
            P("row", "col"),
        ),
        out_specs=P(("groups", "row"), "col"),
        check_vma=False,
    )
```

```python
import functools

import jax
import jax.numpy as jnp
from jax import lax
from jax.experimental import pallas as pl
from jax.experimental.pallas import tpu as pltpu
from jax.sharding import PartitionSpec as P

SIDE = 128
DEPTH = 2
ITEMS = 8
TRIP = ITEMS * DEPTH
HELD = 2
F32 = jnp.float32
BF16 = jnp.bfloat16


def round_up(n, unit):
    return -(-n // unit) * unit


def kept_items(mask):
    deep, wide = mask.shape
    kept = (mask != 0).astype(jnp.int32).T
    row = jnp.arange(deep)
    before = jnp.sum(jnp.where(row[None, :, None] > row[None, None, :], kept[:, None, :], 0), axis=2)
    filled = round_up(jnp.sum(kept, axis=1), DEPTH)
    column = jnp.arange(wide)
    ends = jnp.sum(jnp.where(column[:, None] >= column[None, :], filled[None, :], 0), axis=1)
    place = jnp.where(kept != 0, (ends - filled)[:, None] + before, -1)
    spots = jnp.arange(round_up(wide * round_up(deep, DEPTH), TRIP))
    rows = deep + jnp.sum(
        jnp.where(place[None] == spots[:, None, None], row[None, None, :] - deep, 0), axis=(1, 2)
    )
    items = jnp.arange(spots.shape[0] // DEPTH + 1)
    columns = jnp.sum((ends[None, :] <= items[:, None] * DEPTH).astype(jnp.int32), axis=1)
    trips = round_up(jnp.max(ends[None, :] + items[:, None], axis=1) - items, TRIP) // (TRIP)
    columns = jnp.where(items == items.shape[0] - 1, trips, jnp.minimum(columns, wide - 1))
    return rows.astype(jnp.int32), columns.astype(jnp.int32)


def trips_of(columns):
    return columns[columns.shape[0] - 1]


def block_of(i):
    return pl.ds(pl.multiple_of(i * SIDE, SIDE), SIDE)


def trip_blocks(ref, k):
    return ref.at[pl.ds(pl.multiple_of(k * TRIP * SIDE, TRIP * SIDE), TRIP * SIDE), :]


def start_trip(k, rows, columns, weight, into, sem):
    deep = weight.shape[0] // SIDE
    for t in range(TRIP):
        i = rows[k * TRIP + t]
        pltpu.make_async_copy(
            weight.at[block_of(jnp.where(i == deep, 0, i)), block_of(columns[k * ITEMS + t // DEPTH])],
            into.at[pl.ds(t * SIDE, SIDE), :],
            sem,
        ).start()


def wait_trip(into, sem):
    pltpu.make_async_copy(into, into, sem).wait()


def multiply_trip(k, rows, columns, held, blocks, total):
    deep = DEPTH * SIDE
    for t in range(ITEMS):
        item = k * ITEMS + t
        lhs = jnp.concatenate([held[:, block_of(rows[item * DEPTH + d])] for d in range(DEPTH)], axis=1)
        rhs = blocks[pl.ds(t * deep, deep), :]
        total[:, block_of(columns[item])] += jnp.dot(lhs, rhs, preferred_element_type=F32)


def multiply(rows, columns, packed, weight, held, spill, sem, total):
    def ready(k, _):
        multiply_trip(k, rows, columns, held, trip_blocks(packed, k), total)
        return 0

    def beyond(k, _):
        start_trip(k, rows, columns, weight, spill, sem)
        wait_trip(spill, sem)
        multiply_trip(k, rows, columns, held, spill, total)
        return 0

    trips = trips_of(columns)
    room = packed.shape[0] // (TRIP * SIDE)
    lax.fori_loop(0, jnp.minimum(trips, room), ready, 0)
    lax.fori_loop(room, jnp.maximum(trips, room), beyond, 0)


SPILL = [pltpu.VMEM((TRIP * SIDE, SIDE), BF16), pltpu.SemaphoreType.DMA(())]
SMEM = pl.BlockSpec(memory_space=pltpu.SMEM)
VMEM = pl.BlockSpec(memory_space=pltpu.VMEM)
HBM = pl.BlockSpec(memory_space=pltpu.HBM)


def packed_trips(columns, packed):
    return jnp.minimum(trips_of(columns), packed.shape[0] // (TRIP * SIDE))


def start_packing(rows, columns, weight, packed, sem):
    def start(k, _):
        start_trip(k, rows, columns, weight, trip_blocks(packed, k), sem)
        return 0

    lax.fori_loop(0, packed_trips(columns, packed), start, 0)


def wait_packing(columns, packed, sem):
    def wait(k, _):
        wait_trip(trip_blocks(packed, k), sem)
        return 0

    lax.fori_loop(0, packed_trips(columns, packed), wait, 0)


def packed_shape(items):
    return jax.ShapeDtypeStruct((-(-items[0].shape[0] // (TRIP * HELD)) * TRIP * SIDE, SIDE), BF16)


def pack_kernel(count, *refs):
    lists, weights, packed, sems = refs[: 2 * count], refs[2 * count : 3 * count], refs[3 * count : 4 * count], refs[-1]
    for w in range(count):
        start_packing(*lists[2 * w : 2 * w + 2], weights[w], packed[w], sems.at[w])
    for w in range(count):
        wait_packing(lists[2 * w + 1], packed[w], sems.at[w])


def pack(weights, items):
    count = len(weights)
    return pl.pallas_call(
        functools.partial(pack_kernel, count),
        out_shape=[packed_shape(one) for one in items],
        in_specs=[SMEM] * (2 * count) + [HBM] * count,
        out_specs=[VMEM] * count,
        scratch_shapes=[pltpu.SemaphoreType.DMA((count,))],
        compiler_params=pltpu.CompilerParams(vmem_limit_bytes=1 << 20),
        cost_estimate=pl.CostEstimate(
            flops=0, bytes_accessed=sum(2 * weight.size for weight in weights), transcendentals=0
        ),
    )(*(one for pair in items for one in pair), *weights)


def tokens_kernel(places, packs, *refs):
    lists, refs = refs[:4], refs[4:]
    pieces, refs = refs[: len(places)], refs[len(places) :]
    packed, (gate, up), refs = refs[:2], refs[2:4], refs[4:]
    if packs:
        rows, columns, down, out, down_packed, held, sems, spill, sem, pack_sem = refs
    else:
        out, held, sems, spill, sem = refs
    deep, width = gate.shape
    copies = [
        pltpu.make_async_copy(piece, held.at[pl.ds(row, piece.shape[0]), pl.ds(column, piece.shape[1])], sems.at[k])
        for k, (piece, (row, column)) in enumerate(zip(pieces, places))
    ]
    for copy in copies:
        copy.start()
    if packs:
        start_packing(rows, columns, down, down_packed, pack_sem)
    held[:, deep:] = jnp.zeros((held.shape[0], SIDE), BF16)
    out[...] = jnp.zeros(out.shape, F32)
    for copy in copies:
        copy.wait()
    for w, weight in enumerate((gate, up)):
        total = out.at[:, pl.ds(w * width, width)]
        multiply(*lists[2 * w : 2 * w + 2], packed[w], weight, held, spill, sem, total)
    if packs:
        wait_packing(columns, down_packed, pack_sem)


def tokens_product(items, pieces, places, packed, gate, up, to_pack=()):
    rows = max(row + piece.shape[0] for piece, (row, _) in zip(pieces, places))
    deep, width = gate.shape
    return pl.pallas_call(
        functools.partial(tokens_kernel, places, bool(to_pack)),
        out_shape=[jax.ShapeDtypeStruct((rows, 2 * width), F32)] + ([packed_shape(to_pack)] if to_pack else []),
        in_specs=[SMEM] * 4 + [VMEM] * (len(pieces) + 2) + [HBM] * 2 + ([SMEM, SMEM, HBM] if to_pack else []),
        out_specs=[VMEM] * (2 if to_pack else 1),
        scratch_shapes=[pltpu.VMEM((rows, deep + SIDE), BF16), pltpu.SemaphoreType.DMA((len(pieces),)), *SPILL]
        + ([pltpu.SemaphoreType.DMA(())] if to_pack else []),
        compiler_params=pltpu.CompilerParams(vmem_limit_bytes=6 << 20),
        cost_estimate=pl.CostEstimate(
            flops=16 * rows * deep * width, bytes_accessed=16 * deep * width, transcendentals=0
        ),
    )(*(one for pair in items for one in pair), *pieces, *packed, gate, up, *to_pack)


def down_kernel(groups, opposite, rows, columns, *refs):
    sums, refs = refs[: 2 * groups], refs[2 * groups :]
    if opposite:
        packed, down, on, back, total, held, spill, sem = refs
    else:
        packed, down, total, held, spill, sem = refs
    deep = down.shape[0]
    held[:, deep:] = jnp.zeros((held.shape[0], SIDE), BF16)
    total[...] = jnp.zeros(total.shape, F32)
    at = 0
    for g in range(groups):
        mine, other = sums[2 * g : 2 * g + 2]

        def some(s, _, at=at, mine=mine, other=other):
            here = pl.ds(pl.multiple_of(s * 16, 16), 16)
            value = mine[here, :] + other[here, :]
            silu = value[:, :deep] / (1.0 + jnp.exp(-value[:, :deep]))
            held[pl.ds(pl.multiple_of(at + s * 16, 16), 16), pl.ds(0, deep)] = (silu * value[:, deep:]).astype(BF16)
            return 0

        lax.fori_loop(0, mine.shape[0] // 16, some, 0)
        at += mine.shape[0]
    multiply(rows, columns, packed, down, held, spill, sem, total)
    if opposite:
        half = on.shape[1]
        on[...] = total[:, pl.ds(0, half)].astype(BF16)
        back[...] = total[:, pl.ds(half, half)].astype(BF16)


def down_product(items, sums, packed, down, opposite):
    deep, width = down.shape
    groups = len(sums)
    rows = sum(mine.shape[0] for mine, _ in sums)
    whole = pltpu.VMEM((rows, width), F32)
    half = jax.ShapeDtypeStruct((rows, width // 2), BF16)
    return pl.pallas_call(
        functools.partial(down_kernel, groups, opposite),
        out_shape=(half, half) if opposite else jax.ShapeDtypeStruct((rows, width), F32),
        in_specs=[SMEM] * 2 + [VMEM] * (2 * groups + 1) + [HBM],
        out_specs=(VMEM, VMEM) if opposite else VMEM,
        scratch_shapes=([whole] if opposite else []) + [pltpu.VMEM((rows, deep + SIDE), BF16), *SPILL],
        compiler_params=pltpu.CompilerParams(vmem_limit_bytes=6 << 20),
        cost_estimate=pl.CostEstimate(
            flops=rows * deep * width * 2, bytes_accessed=deep * width * 2, transcendentals=rows * deep
        ),
    )(*items, *(part for pair in sums for part in pair), packed, down)


def ring_of(n):
    order = list(range(n)) if n > 8 else list(range(0, n, 2)) + list(range(n - 1, 0, -2))
    onward = [(order[k], order[(k + 1) % n]) for k in range(n)]
    return onward, [(b, a) for a, b in onward]


def tie(values, *before):
    return lax.optimization_barrier((values, before))[0]


STREAMS = 2


def scatter(opposite, late, onward, back, n):
    far = n // 2
    few = opposite[0].shape[0] // STREAMS
    half = opposite[0].shape[1]
    cut = [slice(s * few, (s + 1) * few) for s in range(STREAMS)]
    sent = [[block[rows] for block in opposite] for rows in cut]
    last = None
    for k in range(far - 1, -1, -1):
        blocks = late(k, last)
        for s, rows in enumerate(cut):
            on, ba = (lax.ppermute(block, "row", way) for block, way in zip(sent[s], (onward, back)))
            if k == 0:
                on, ba = tie((on, ba), last)
                last = sent[s] = ((blocks[0][rows] + on.astype(F32) + ba.astype(F32)).astype(BF16),)
                continue
            both = []
            for side, (sum_, block) in enumerate(((on, blocks[1]), (ba, blocks[0]))):
                sum_ = (sum_ if last is None else tie(sum_, last)).astype(F32)
                block = block[rows]
                if k < far - 1:
                    block = block + sum_
                elif side == 0:
                    block = jnp.concatenate((block[:, :half] + sum_, block[:, half:]), axis=1)
                else:
                    block = jnp.concatenate((block[:, :half], block[:, half:] + sum_), axis=1)
                last = block.astype(BF16)
                both.append(last)
            sent[s] = both
    return jnp.concatenate([block for (block,) in sent], axis=0)


def body(n, tokens, gate, up, down, gate_mask, up_mask, down_mask):
    onward, back = ring_of(n)
    swap = [(0, 1), (1, 0)]
    far = n // 2
    half = tokens.shape[1] // 2
    gate_items, up_items, down_items = kept_items(gate_mask), kept_items(up_mask), kept_items(down_mask)
    rows = tokens.shape[0]
    def product(group, to_pack=()):
        pieces, places = [], []
        at = 0
        for k in group:
            for piece in steps[k]:
                pieces.append(piece)
                places.append((at, 0))
                at += rows
        if group[-1] == far:
            places[-2:] = [(at - 2 * rows, 0), (at - 2 * rows, half)]
        mine, *more = tokens_product((gate_items, up_items), pieces, places, packed, gate, up, to_pack)
        return mine, lax.ppermute(mine, "col", swap), *more

    gate, up, down = (pltpu.with_memory_space_constraint(w, pltpu.HBM) for w in (gate, up, down))
    packed = pack((gate, up), (gate_items, up_items))
    behind = ahead = tokens
    steps = [(tokens,)]
    sums = []
    for k in range(1, far + 1):
        if k == 3:
            *first, down_packed = product((0, 1), (*down_items, down))
            sums.append(tuple(first))
        elif k > 3:
            sums.append(product((k - 2,)))
        if k > 2:
            behind, ahead = tie(behind, sums[-1][0]), tie(ahead, sums[-1][0])
        if k == far:
            behind, ahead = behind[:, :half], ahead[:, half:]
        behind, ahead = lax.ppermute(behind, "row", onward), lax.ppermute(ahead, "row", back)
        steps.append((behind, ahead))
    sums.append(product((far - 1,)))
    steps[far] = tie(steps[far], sums[-1][0])
    sums.append(product((far,)))
    near = {}

    def late(k, sent):
        if k not in near:
            group = sums[max(k - 1, 0)]
            parts = down_product(down_items, [group if sent is None else tie(group, sent)], down_packed, down, False)
            for i, block in enumerate(((0,), (1, 2)) if k < 2 else ((0, 1),)):
                near[i if k < 2 else k] = [parts[j * rows : (j + 1) * rows] for j in block]
        return near[k]

    opposite = tie(sums[-1], *(other for _, other in sums[:-2]))
    return scatter(down_product(down_items, [opposite], down_packed, down, True), late, onward, back, n)


def solution(mesh):
    return jax.shard_map(
        functools.partial(body, mesh.shape["row"]),
        mesh=mesh,
        in_specs=(
            P(("groups", "row"), "col"),
            P("col", "row"),
            P("col", "row"),
            P("row", "col"),
            P("col", "row"),
            P("col", "row"),
            P("row", "col"),
        ),
        out_specs=P(("groups", "row"), "col"),
        check_vma=False,
    )
```

```python
import functools

import jax
import jax.numpy as jnp
from jax import lax
from jax.experimental import pallas as pl
from jax.experimental.pallas import tpu as pltpu
from jax.sharding import PartitionSpec as P

SIDE = 128
DEPTH = 2
ITEMS = 20
TRIP = ITEMS * DEPTH
HELD = 2
F32 = jnp.float32
BF16 = jnp.bfloat16


def round_up(n, unit):
    return -(-n // unit) * unit


def kept_items(mask):
    deep, wide = mask.shape
    kept = (mask != 0).astype(jnp.int32).T
    row = jnp.arange(deep)
    before = jnp.sum(jnp.where(row[None, :, None] > row[None, None, :], kept[:, None, :], 0), axis=2)
    filled = round_up(jnp.sum(kept, axis=1), DEPTH)
    column = jnp.arange(wide)
    ends = jnp.sum(jnp.where(column[:, None] >= column[None, :], filled[None, :], 0), axis=1)
    place = jnp.where(kept != 0, (ends - filled)[:, None] + before, -1)
    spots = jnp.arange(round_up(wide * round_up(deep, DEPTH), TRIP))
    rows = deep + jnp.sum(
        jnp.where(place[None] == spots[:, None, None], row[None, None, :] - deep, 0), axis=(1, 2)
    )
    items = jnp.arange(spots.shape[0] // DEPTH + 1)
    columns = jnp.sum((ends[None, :] <= items[:, None] * DEPTH).astype(jnp.int32), axis=1)
    trips = round_up(jnp.max(ends[None, :] + items[:, None], axis=1) - items, TRIP) // (TRIP)
    columns = jnp.where(items == items.shape[0] - 1, trips, jnp.minimum(columns, wide - 1))
    return rows.astype(jnp.int32), columns.astype(jnp.int32)


def trips_of(columns):
    return columns[columns.shape[0] - 1]


def block_of(i):
    return pl.ds(pl.multiple_of(i * SIDE, SIDE), SIDE)


def trip_blocks(ref, k):
    return ref.at[pl.ds(pl.multiple_of(k * TRIP * SIDE, TRIP * SIDE), TRIP * SIDE), :]


def start_trip(k, rows, columns, weight, into, sem):
    deep = weight.shape[0] // SIDE
    for t in range(TRIP):
        i = rows[k * TRIP + t]
        pltpu.make_async_copy(
            weight.at[block_of(jnp.where(i == deep, 0, i)), block_of(columns[k * ITEMS + t // DEPTH])],
            into.at[pl.ds(t * SIDE, SIDE), :],
            sem,
        ).start()


def wait_trip(into, sem):
    pltpu.make_async_copy(into, into, sem).wait()


def multiply_trip(k, rows, columns, held, blocks, total):
    deep = DEPTH * SIDE
    for t in range(ITEMS):
        item = k * ITEMS + t
        lhs = jnp.concatenate([held[:, block_of(rows[item * DEPTH + d])] for d in range(DEPTH)], axis=1)
        rhs = blocks[pl.ds(t * deep, deep), :]
        total[:, block_of(columns[item])] += jnp.dot(lhs, rhs, preferred_element_type=F32)


def multiply(rows, columns, packed, weight, held, spill, sem, total):
    def ready(k, _):
        multiply_trip(k, rows, columns, held, trip_blocks(packed, k), total)
        return 0

    def beyond(k, _):
        start_trip(k, rows, columns, weight, spill, sem)
        wait_trip(spill, sem)
        multiply_trip(k, rows, columns, held, spill, total)
        return 0

    trips = trips_of(columns)
    room = packed.shape[0] // (TRIP * SIDE)
    lax.fori_loop(0, jnp.minimum(trips, room), ready, 0)
    lax.fori_loop(room, jnp.maximum(trips, room), beyond, 0)


SPILL = [pltpu.VMEM((TRIP * SIDE, SIDE), BF16), pltpu.SemaphoreType.DMA(())]
SMEM = pl.BlockSpec(memory_space=pltpu.SMEM)
VMEM = pl.BlockSpec(memory_space=pltpu.VMEM)
HBM = pl.BlockSpec(memory_space=pltpu.HBM)


def packed_trips(columns, packed):
    return jnp.minimum(trips_of(columns), packed.shape[0] // (TRIP * SIDE))


def start_packing(rows, columns, weight, packed, sem):
    def start(k, _):
        start_trip(k, rows, columns, weight, trip_blocks(packed, k), sem)
        return 0

    lax.fori_loop(0, packed_trips(columns, packed), start, 0)


def wait_packing(columns, packed, sem):
    def wait(k, _):
        wait_trip(trip_blocks(packed, k), sem)
        return 0

    lax.fori_loop(0, packed_trips(columns, packed), wait, 0)


def packed_shape(items):
    return jax.ShapeDtypeStruct((-(-items[0].shape[0] // (TRIP * HELD)) * TRIP * SIDE, SIDE), BF16)


def pack_kernel(count, *refs):
    lists, weights, packed, sems = refs[: 2 * count], refs[2 * count : 3 * count], refs[3 * count : 4 * count], refs[-1]
    for w in range(count):
        start_packing(*lists[2 * w : 2 * w + 2], weights[w], packed[w], sems.at[w])
    for w in range(count):
        wait_packing(lists[2 * w + 1], packed[w], sems.at[w])


def pack(weights, items):
    count = len(weights)
    return pl.pallas_call(
        functools.partial(pack_kernel, count),
        out_shape=[packed_shape(one) for one in items],
        in_specs=[SMEM] * (2 * count) + [HBM] * count,
        out_specs=[VMEM] * count,
        scratch_shapes=[pltpu.SemaphoreType.DMA((count,))],
        compiler_params=pltpu.CompilerParams(vmem_limit_bytes=1 << 20),
        cost_estimate=pl.CostEstimate(
            flops=0, bytes_accessed=sum(2 * weight.size for weight in weights), transcendentals=0
        ),
    )(*(one for pair in items for one in pair), *weights)


def tokens_kernel(places, packs, *refs):
    lists, refs = refs[:4], refs[4:]
    pieces, refs = refs[: len(places)], refs[len(places) :]
    packed, (gate, up), refs = refs[:2], refs[2:4], refs[4:]
    if packs:
        rows, columns, down, out, down_packed, held, sems, spill, sem, pack_sem = refs
    else:
        out, held, sems, spill, sem = refs
    deep, width = gate.shape
    copies = [
        pltpu.make_async_copy(piece, held.at[pl.ds(row, piece.shape[0]), pl.ds(column, piece.shape[1])], sems.at[k])
        for k, (piece, (row, column)) in enumerate(zip(pieces, places))
    ]
    for copy in copies:
        copy.start()
    if packs:
        start_packing(rows, columns, down, down_packed, pack_sem)
    held[:, deep:] = jnp.zeros((held.shape[0], SIDE), BF16)
    out[...] = jnp.zeros(out.shape, F32)
    for copy in copies:
        copy.wait()
    for w, weight in enumerate((gate, up)):
        total = out.at[:, pl.ds(w * width, width)]
        multiply(*lists[2 * w : 2 * w + 2], packed[w], weight, held, spill, sem, total)
    if packs:
        wait_packing(columns, down_packed, pack_sem)


def tokens_product(items, pieces, places, packed, gate, up, to_pack=()):
    rows = max(row + piece.shape[0] for piece, (row, _) in zip(pieces, places))
    deep, width = gate.shape
    return pl.pallas_call(
        functools.partial(tokens_kernel, places, bool(to_pack)),
        out_shape=[jax.ShapeDtypeStruct((rows, 2 * width), F32)] + ([packed_shape(to_pack)] if to_pack else []),
        in_specs=[SMEM] * 4 + [VMEM] * (len(pieces) + 2) + [HBM] * 2 + ([SMEM, SMEM, HBM] if to_pack else []),
        out_specs=[VMEM] * (2 if to_pack else 1),
        scratch_shapes=[pltpu.VMEM((rows, deep + SIDE), BF16), pltpu.SemaphoreType.DMA((len(pieces),)), *SPILL]
        + ([pltpu.SemaphoreType.DMA(())] if to_pack else []),
        compiler_params=pltpu.CompilerParams(vmem_limit_bytes=6 << 20),
        cost_estimate=pl.CostEstimate(
            flops=16 * rows * deep * width, bytes_accessed=16 * deep * width, transcendentals=0
        ),
    )(*(one for pair in items for one in pair), *pieces, *packed, gate, up, *to_pack)


def down_kernel(groups, opposite, rows, columns, *refs):
    sums, refs = refs[: 2 * groups], refs[2 * groups :]
    if opposite:
        packed, down, on, back, total, held, spill, sem = refs
    else:
        packed, down, total, held, spill, sem = refs
    deep = down.shape[0]
    held[:, deep:] = jnp.zeros((held.shape[0], SIDE), BF16)
    total[...] = jnp.zeros(total.shape, F32)
    at = 0
    for g in range(groups):
        mine, other = sums[2 * g : 2 * g + 2]

        def some(s, _, at=at, mine=mine, other=other):
            here = pl.ds(pl.multiple_of(s * 16, 16), 16)
            value = mine[here, :] + other[here, :]
            silu = value[:, :deep] / (1.0 + jnp.exp(-value[:, :deep]))
            held[pl.ds(pl.multiple_of(at + s * 16, 16), 16), pl.ds(0, deep)] = (silu * value[:, deep:]).astype(BF16)
            return 0

        lax.fori_loop(0, mine.shape[0] // 16, some, 0)
        at += mine.shape[0]
    multiply(rows, columns, packed, down, held, spill, sem, total)
    if opposite:
        half = on.shape[1]
        on[...] = total[:, pl.ds(0, half)].astype(BF16)
        back[...] = total[:, pl.ds(half, half)].astype(BF16)


def down_product(items, sums, packed, down, opposite):
    deep, width = down.shape
    groups = len(sums)
    rows = sum(mine.shape[0] for mine, _ in sums)
    whole = pltpu.VMEM((rows, width), F32)
    half = jax.ShapeDtypeStruct((rows, width // 2), BF16)
    return pl.pallas_call(
        functools.partial(down_kernel, groups, opposite),
        out_shape=(half, half) if opposite else jax.ShapeDtypeStruct((rows, width), F32),
        in_specs=[SMEM] * 2 + [VMEM] * (2 * groups + 1) + [HBM],
        out_specs=(VMEM, VMEM) if opposite else VMEM,
        scratch_shapes=([whole] if opposite else []) + [pltpu.VMEM((rows, deep + SIDE), BF16), *SPILL],
        compiler_params=pltpu.CompilerParams(vmem_limit_bytes=6 << 20),
        cost_estimate=pl.CostEstimate(
            flops=rows * deep * width * 2, bytes_accessed=deep * width * 2, transcendentals=rows * deep
        ),
    )(*items, *(part for pair in sums for part in pair), packed, down)


def ring_of(n):
    order = list(range(n)) if n > 8 else list(range(0, n, 2)) + list(range(n - 1, 0, -2))
    onward = [(order[k], order[(k + 1) % n]) for k in range(n)]
    return onward, [(b, a) for a, b in onward]


def tie(values, *before):
    return lax.optimization_barrier((values, before))[0]


STREAMS = 2


def scatter(opposite, late, onward, back, n):
    far = n // 2
    few = opposite[0].shape[0] // STREAMS
    half = opposite[0].shape[1]
    cut = [slice(s * few, (s + 1) * few) for s in range(STREAMS)]
    sent = [[block[rows] for block in opposite] for rows in cut]
    last = None
    for k in range(far - 1, -1, -1):
        blocks = late(k, last)
        for s, rows in enumerate(cut):
            on, ba = (lax.ppermute(block, "row", way) for block, way in zip(sent[s], (onward, back)))
            if k == 0:
                on, ba = tie((on, ba), last)
                last = sent[s] = ((blocks[0][rows] + on.astype(F32) + ba.astype(F32)).astype(BF16),)
                continue
            both = []
            for side, (sum_, block) in enumerate(((on, blocks[1]), (ba, blocks[0]))):
                sum_ = (sum_ if last is None else tie(sum_, last)).astype(F32)
                block = block[rows]
                if k < far - 1:
                    block = block + sum_
                elif side == 0:
                    block = jnp.concatenate((block[:, :half] + sum_, block[:, half:]), axis=1)
                else:
                    block = jnp.concatenate((block[:, :half], block[:, half:] + sum_), axis=1)
                last = block.astype(BF16)
                both.append(last)
            sent[s] = both
    return jnp.concatenate([block for (block,) in sent], axis=0)


def body(n, tokens, gate, up, down, gate_mask, up_mask, down_mask):
    onward, back = ring_of(n)
    swap = [(0, 1), (1, 0)]
    far = n // 2
    half = tokens.shape[1] // 2
    gate_items, up_items, down_items = kept_items(gate_mask), kept_items(up_mask), kept_items(down_mask)
    rows = tokens.shape[0]
    def product(group, to_pack=()):
        pieces, places = [], []
        at = 0
        for k in group:
            for piece in steps[k]:
                pieces.append(piece)
                places.append((at, 0))
                at += rows
        if group[-1] == far:
            places[-2:] = [(at - 2 * rows, 0), (at - 2 * rows, half)]
        mine, *more = tokens_product((gate_items, up_items), pieces, places, packed, gate, up, to_pack)
        return mine, lax.ppermute(mine, "col", swap), *more

    gate, up, down = (pltpu.with_memory_space_constraint(w, pltpu.HBM) for w in (gate, up, down))
    packed = pack((gate, up), (gate_items, up_items))
    behind = ahead = tokens
    steps = [(tokens,)]
    sums = []
    for k in range(1, far + 1):
        if k == 3:
            *first, down_packed = product((0, 1), (*down_items, down))
            sums.append(tuple(first))
        elif k > 3:
            sums.append(product((k - 2,)))
        if k > 2:
            behind, ahead = tie(behind, sums[-1][0]), tie(ahead, sums[-1][0])
        if k == far:
            behind, ahead = behind[:, :half], ahead[:, half:]
        behind, ahead = lax.ppermute(behind, "row", onward), lax.ppermute(ahead, "row", back)
        steps.append((behind, ahead))
    sums.append(product((far - 1,)))
    steps[far] = tie(steps[far], sums[-1][0])
    sums.append(product((far,)))
    near = {}

    def late(k, sent):
        if k not in near:
            group = sums[max(k - 1, 0)]
            parts = down_product(down_items, [group if sent is None else tie(group, sent)], down_packed, down, False)
            for i, block in enumerate(((0,), (1, 2)) if k < 2 else ((0, 1),)):
                near[i if k < 2 else k] = [parts[j * rows : (j + 1) * rows] for j in block]
        return near[k]

    opposite = tie(sums[-1], *(other for _, other in sums[:-2]))
    return scatter(down_product(down_items, [opposite], down_packed, down, True), late, onward, back, n)


def solution(mesh):
    return jax.shard_map(
        functools.partial(body, mesh.shape["row"]),
        mesh=mesh,
        in_specs=(
            P(("groups", "row"), "col"),
            P("col", "row"),
            P("col", "row"),
            P("row", "col"),
            P("col", "row"),
            P("col", "row"),
            P("row", "col"),
        ),
        out_specs=P(("groups", "row"), "col"),
        check_vma=False,
    )
```
